1024 devices in a mesh: dp: 32 (over z_lo, y), expert: 32 (over x, z_hi, core).
Axes of the slice: x: 4, y: 4, z: 32 (z_hi: 4, z_lo: 8; z = z_hi * 8 + z_lo), core: 2. Of those that a mesh axis runs over, the one named last changes fastest.
Arguments:
- tokens: bfloat16 [131072, 2048], P(('dp', 'expert')), may hold values from -6 to 6
- expert_ids: int32 [131072, 2], P(('dp', 'expert')), may hold values from 0 to 15, all different within a row
- copy_choice: int32 [131072, 2], P(('dp', 'expert')), may hold values from 0 to 1
- gate_weights: float32 [131072, 2], P(('dp', 'expert')), may hold values from 0.05 to 1
- w_gate: bfloat16 [2048, 24576], P(None, 'expert'), may hold values from -0.125 to 0.125
- w_up: bfloat16 [2048, 24576], P(None, 'expert'), may hold values from -0.125 to 0.125
- w_down: bfloat16 [24576, 2048], P('expert'), may hold values from -0.15625 to 0.15625
Outputs:
- moe_out: bfloat16 [131072, 2048], P(('dp', 'expert'))
- expert_load: float32 [16], replicated
The draws below stay inside these ranges and needn't reach their ends.
Inputs may be any that keep to these rules, and one draw needn't show every extreme that they name: `expert_ids`: the 2 experts of a token are distinct.
All inputs are finite; a program needn't handle non-finite values.
Results may differ from the reference program's by a relative error of at most 0.0049.
Values may be sent and summed in bfloat16 or wider, within the bound.
A program may use at most 64 MiB of HBM per device.

```python
import math
import jax
import jax.numpy as jnp
from jax import lax

D = 2048
FF = 1536
TOK_DEV = 128
EXPERTS = 16
TOPK = 2
CAP = 8
TOKENS = 131072
N_DP = 32
N_EXPERT = 32


def touch_ends(array, key, smallest, top_value):
    longest = array.shape.index(max(array.shape))
    spots = []
    for shift in (0, 1):
        where = [jax.random.randint(jax.random.fold_in(key, axis), (), 0, length) for axis, length in enumerate(array.shape)]
        where[longest] = (where[longest] + shift) % array.shape[longest]
        spots.append(tuple(where))
    return array.at[spots[0]].set(smallest).at[spots[1]].set(top_value)


def levels(rng, shape, cuts, low, top_value):
    gain, own = 1.0, jax.random.fold_in(rng, 6)
    for dim, blocks in cuts:
        heights = jnp.exp(jax.random.uniform(jax.random.fold_in(own, dim), (blocks,), jnp.float32, low / len(cuts), top_value / len(cuts)))
        gain = gain * jnp.repeat(heights, shape[dim] // blocks).reshape([-1 if axis == dim else 1 for axis in range(len(shape))])
    return gain


def picks_of(stream_key, rows, count, top, lift):
    order = jax.random.permutation(jax.random.fold_in(stream_key, 1), count)
    favour = order
    for power in range(3):
        favour = favour * favour // count
    favour = favour * lift // count
    chance = jax.random.randint(jax.random.fold_in(stream_key, 2), (rows, count), 0, 4096) + favour
    fixed_rows = jax.random.permutation(jax.random.fold_in(stream_key, 3), rows)[jnp.arange(count) % rows]
    chance = jnp.where(jnp.arange(rows)[:, None] == fixed_rows[None, :], 1 << 14, chance)
    score = chance * count + jnp.arange(count)
    return lax.top_k(score.astype(jnp.int32), top)[1].astype(jnp.int32)


def noise(rng, dims, spread, limit, cuts=(), held_as=jnp.bfloat16):
    loudness = levels(rng, dims, cuts, -0.22, 0.18) if cuts else 1.0
    result = jax.random.normal(rng, dims, jnp.float32) * spread * loudness
    return jnp.minimum(jnp.maximum(result, -limit), limit).astype(held_as)


def setup_inputs(seed: int = 0) -> dict:
    arg_keys = jax.random.split(jax.random.key(seed), 8)
    tokens = noise(arg_keys[0], (TOKENS, D), 1.0, 6.0, ((0, 1024),))
    expert_ids = picks_of(arg_keys[1], TOKENS, EXPERTS, TOPK, 2048)
    copy_choice = touch_ends(jax.random.randint(arg_keys[2], (TOKENS, TOPK), 0, 2), jax.random.fold_in(arg_keys[2], 1), 0, 1).astype(jnp.int32)
    gate_weights = jnp.clip(jnp.exp(math.log(1.0) - 2.9957323 * jax.random.uniform(arg_keys[3], (TOKENS, TOPK), jnp.float32) ** levels(arg_keys[3], (TOKENS, TOPK), ((0, 1024),), -0.2, 0.2)), 0.05, 1.0)
    w_gate = noise(arg_keys[4], (D, EXPERTS * FF), D ** -0.5, 0.125, ((1, 32),))
    w_up = noise(arg_keys[5], (D, EXPERTS * FF), D ** -0.5, 0.125, ((1, 32),))
    w_down = noise(arg_keys[6], (EXPERTS * FF, D), FF ** -0.5, 0.15625, ((0, 32),))
    return {"tokens": tokens, "expert_ids": expert_ids, "copy_choice": copy_choice, "gate_weights": gate_weights, "w_gate": w_gate, "w_up": w_up, "w_down": w_down}


def expert_pass(inputs, weight_gate, weight_up, weight_down):
    gate_act = jnp.dot(inputs, weight_gate, preferred_element_type=jnp.float32)
    up_act = jnp.dot(inputs, weight_up, preferred_element_type=jnp.float32)
    hidden = (jax.nn.silu(gate_act) * up_act).astype(jnp.bfloat16)
    return jnp.dot(hidden, weight_down, preferred_element_type=jnp.float32)


def reference(tokens, expert_ids, copy_choice, gate_weights, w_gate, w_up, w_down):
    devices = N_DP * N_EXPERT
    per_block = TOK_DEV * TOPK
    route_keys = (expert_ids * 2 + copy_choice).reshape(devices, per_block)
    onehot = (route_keys[:, :, None] == jnp.arange(2 * EXPERTS, dtype=jnp.int32)[None, None, :]).astype(jnp.int32)
    before = jnp.cumsum(onehot, axis=1) - onehot
    slot_rank = jnp.sum(before * onehot, axis=2)
    retained = slot_rank < CAP
    weighted = jnp.where(retained.reshape(TOKENS, TOPK), gate_weights, jnp.zeros_like(gate_weights))

    block_ids = jnp.arange(devices, dtype=jnp.int32)[:, None]
    route_pos = jnp.arange(per_block, dtype=jnp.int32)[None, :]
    token_index = block_ids * TOK_DEV + route_pos // TOPK
    flat_route = block_ids * per_block + route_pos
    place = jnp.where(retained, route_keys * CAP + slot_rank, 2 * EXPERTS * CAP)
    slot_count = 2 * EXPERTS * CAP + 1
    slot_token = jnp.full((devices, slot_count), -1, jnp.int32)
    slot_token = slot_token.at[block_ids, place].set(token_index)
    slot_route = jnp.full((devices, slot_count), -1, jnp.int32)
    slot_route = slot_route.at[block_ids, place].set(flat_route)
    slot_token = slot_token[:, :-1].reshape(devices, EXPERTS, 2 * CAP)
    slot_route = slot_route[:, :-1].reshape(devices, EXPERTS, 2 * CAP)
    flat_gate = weighted.reshape(-1)

    def one_expert(running, expert_id):
        start = (expert_id * FF).astype(jnp.int32)
        weight_gate = lax.dynamic_slice_in_dim(w_gate, start, FF, 1)
        weight_up = lax.dynamic_slice_in_dim(w_up, start, FF, 1)
        weight_down = lax.dynamic_slice_in_dim(w_down, start, FF, 0)
        rows_tok = lax.dynamic_index_in_dim(slot_token, expert_id, 1, keepdims=False).reshape(-1)
        rows_route = lax.dynamic_index_in_dim(slot_route, expert_id, 1, keepdims=False).reshape(-1)
        valid = rows_tok >= 0
        safe_tok = jnp.where(valid, rows_tok, 0)
        safe_route = jnp.where(valid, rows_route, 0)
        inputs = jnp.where(valid[:, None], tokens[safe_tok], jnp.zeros((), tokens.dtype))
        share = jnp.where(valid, flat_gate[safe_route], jnp.zeros((), jnp.float32))
        expert_out = expert_pass(inputs, weight_gate, weight_up, weight_down)
        running = running.at[safe_tok].add(share[:, None] * expert_out)
        load = jnp.sum(jnp.where(expert_ids == expert_id, weighted, jnp.zeros_like(weighted)))
        return running, load

    initial = jnp.zeros((TOKENS, D), jnp.float32)
    summed, load_list = lax.scan(one_expert, initial, jnp.arange(EXPERTS, dtype=jnp.int32))
    return summed.astype(jnp.bfloat16), load_list / TOKENS
```

```python
import jax
import jax.numpy as jnp
from jax import lax
from jax.experimental import pallas as pl
from jax.experimental.pallas import tpu as pltpu
from jax.sharding import PartitionSpec as P

MESH = pl.DeviceIdType.MESH

BLOCKS = 4
DEPTH = 8
SIDE = 4
PLANE = SIDE * SIDE
CAP = 8
GU_ROWS = 64
DN_ROWS = 32
N_OWN = 8
PEAK = 32


def routing(ids_ref, copy_ref, gate_ref):
    rows = ids_ref.shape[0]
    lanes = lax.broadcasted_iota(jnp.int32, (rows, 128), 1)
    ids = [ids_ref[:, k : k + 1] for k in (0, 1)]
    copies = [copy_ref[:, k : k + 1] for k in (0, 1)]
    hot = [(lanes == 2 * ids[k] + copies[k]).astype(jnp.float32) for k in (0, 1)]
    earlier = lax.broadcasted_iota(jnp.int32, (rows, rows), 1) < lax.broadcasted_iota(
        jnp.int32, (rows, rows), 0
    )
    before = jnp.dot(
        earlier.astype(jnp.float32).astype(jnp.bfloat16),
        (hot[0] + hot[1]).astype(jnp.bfloat16),
        preferred_element_type=jnp.float32,
    )
    ranks = [
        jnp.sum(before * hot[0], axis=1, keepdims=True),
        jnp.sum((before + hot[0]) * hot[1], axis=1, keepdims=True),
    ]
    routes = []
    for k in (0, 1):
        kept = ranks[k] < float(CAP)
        place = (copies[k] * CAP).astype(jnp.float32) + ranks[k]
        gate = jnp.where(kept, gate_ref[:, k : k + 1], 0.0)
        routes.append((ids[k], place, kept, gate))
    return routes


def load_kernel(ids_ref, copy_ref, gate_ref, out_ref):
    lanes = lax.broadcasted_iota(jnp.int32, (ids_ref.shape[0], 128), 1)
    total = jnp.zeros((1, 128), jnp.float32)
    for expert, _, _, gate in routing(ids_ref, copy_ref, gate_ref):
        total += jnp.sum(jnp.where(lanes == expert, gate, 0.0), axis=0, keepdims=True)
    out_ref[...] = jnp.broadcast_to(total, out_ref.shape)


def moe_kernel(
    tokens_ref, ids_ref, copy_ref, gate_ref, wg_ref, wu_ref, wd_ref, out_ref,
    gu, dn, packed, arrived, result, back, acc,
    own_sem, o_send, o_recv, z_send, z_recv, d_send, d_recv, x_send, x_recv, r_send, r_recv,
):
    dp, ex = lax.axis_index("dp"), lax.axis_index("expert")
    zlo, y = dp // SIDE, lax.rem(dp, SIDE)
    x, b, c = ex // (2 * BLOCKS), lax.rem(ex // 2, BLOCKS), lax.rem(ex, 2)
    me = x * SIDE + y
    first_core = c == 0
    features = tokens_ref.shape[1]
    quarter = dn.shape[1]
    gu_chunks = features // GU_ROWS
    chunks = gu_chunks + quarter // DN_ROWS
    own_rows = features // N_OWN
    own_pieces = N_OWN + quarter // 128
    slots = 2 * CAP

    def at_plane(step):
        z = lax.rem(b * DEPTH + zlo + step + BLOCKS * DEPTH, BLOCKS * DEPTH)
        zb, zl = z // DEPTH, lax.rem(z, DEPTH)
        return (zl * SIDE + y, x * 2 * BLOCKS + zb * 2 + c)

    def at_peer(peer):
        return (zlo * SIDE + lax.rem(peer, SIDE), (peer // SIDE) * 2 * BLOCKS + b * 2 + c)

    def peer_of(i):
        return lax.rem(me + i, PLANE)

    ahead = jnp.where(first_core, 1, -1)
    downstream, upstream = at_plane(ahead), at_plane(-ahead)
    partner = (dp, x * 2 * BLOCKS + b * 2 + 1 - c)

    holder = c == y // 2
    column = pl.multiple_of(lax.rem(y, 2) * quarter, 128)

    def own_copies(p):
        if p < N_OWN:
            rows = pl.ds(p * own_rows, own_rows)
            return [
                pltpu.make_async_copy(
                    w.at[rows, pl.ds(column, quarter)],
                    gu.at[0, rows, pl.ds(k * quarter, quarter)],
                    own_sem.at[2 * p + k],
                )
                for k, w in ((0, wg_ref), (1, wu_ref))
            ]
        at = (p - N_OWN) * 128
        return [
            pltpu.make_async_copy(
                wd_ref.at[pl.ds(column + at, 128), :],
                dn.at[0, pl.ds(at, 128), :],
                own_sem.at[N_OWN + p],
            )
        ]

    def own_to_partner(p):
        ref = gu.at[0, pl.ds(p * own_rows, own_rows)] if p < N_OWN else dn.at[0, pl.ds((p - N_OWN) * 128, 128)]
        return pltpu.make_async_remote_copy(
            ref, ref, o_send.at[p], o_recv.at[p], device_id=partner, device_id_type=MESH
        )

    own_order = []
    for p in range((own_pieces + 1) // 2):
        own_order += [p] if p == own_pieces - 1 - p else [p, own_pieces - 1 - p]

    @pl.when(holder)
    def _():
        for p in own_order:
            for copy in own_copies(p):
                copy.start()

    barrier = pltpu.get_barrier_semaphore()

    def greet(i, carry):
        pl.semaphore_signal(barrier, inc=1, device_id=at_peer(peer_of(i)), device_id_type=MESH)
        return carry

    pl.semaphore_signal(barrier, inc=1, device_id=upstream, device_id_type=MESH)
    pl.semaphore_signal(barrier, inc=1, device_id=partner, device_id_type=MESH)
    lax.fori_loop(1, PLANE, greet, 0)

    routes = routing(ids_ref, copy_ref, gate_ref)
    codes = []
    for expert, place, kept, _ in routes:
        group = lax.rem(b - expert + BLOCKS * SIDE, BLOCKS) * SIDE + expert // BLOCKS
        codes.append(jnp.where(kept, (group * slots).astype(jnp.float32) + place, -1.0))
    n_tokens = tokens_ref.shape[0]
    width = BLOCKS * SIDE * slots
    lanes = lax.broadcasted_iota(jnp.int32, (n_tokens, width), 1)
    plain = lanes.astype(jnp.float32)
    select = jnp.where(plain == codes[0], 1.0, 0.0) + jnp.where(plain == codes[1], 1.0, 0.0)
    rows = jnp.dot(
        select.T.astype(jnp.bfloat16), tokens_ref[...], preferred_element_type=jnp.float32
    ).astype(jnp.bfloat16)
    packed[...] = rows.reshape(packed.shape)

    pl.semaphore_wait(barrier, PLANE + 1)

    @pl.when(holder)
    def _():
        for p in own_order:
            for copy in own_copies(p):
                copy.wait()
            own_to_partner(p).start()

    side = jnp.where(first_core, 1, 3)
    other_side = 4 - side
    last = jnp.where(first_core, zlo == DEPTH - 1, zlo == 0)

    def chunk_at(t, mine=True):
        ascending = first_core if mine else jnp.logical_not(first_core)
        return jnp.where(ascending, t, chunks - 1 - t)

    def on_chunk(chunk, act):
        @pl.when(chunk < gu_chunks)
        def _():
            act(lambda s: gu.at[s, pl.ds(pl.multiple_of(chunk * GU_ROWS, GU_ROWS), GU_ROWS)])

        @pl.when(chunk >= gu_chunks)
        def _():
            at = (chunk - gu_chunks) * DN_ROWS
            act(lambda s: dn.at[s, pl.ds(pl.multiple_of(at, DN_ROWS), DN_ROWS)])

    def along(src, dst, sem):
        return pltpu.make_async_remote_copy(
            src, dst, z_send.at[sem], z_recv.at[sem], device_id=downstream, device_id_type=MESH
        )

    def across(ref, sem):
        return pltpu.make_async_remote_copy(
            ref, ref, d_send.at[sem], d_recv.at[sem], device_id=partner, device_id_type=MESH
        )

    def send_own(t, carry):
        on_chunk(chunk_at(t), lambda view: along(view(0), view(side), t).start())
        return carry

    @pl.when(jnp.logical_and(last, holder))
    def _():
        lax.fori_loop(0, chunks, send_own, 0)

    @pl.when(jnp.logical_and(last, jnp.logical_not(holder)))
    def _():
        per_piece = chunks // own_pieces

        @pl.when(first_core)
        def _():
            for i in range(own_pieces):
                own_to_partner(i).wait_recv()
                lax.fori_loop(i * per_piece, (i + 1) * per_piece, send_own, 0)

        @pl.when(jnp.logical_not(first_core))
        def _():
            for i in range(own_pieces):
                own_to_partner(own_pieces - 1 - i).wait_recv()
                lax.fori_loop(i * per_piece, (i + 1) * per_piece, send_own, 0)

    def to_peer(r, peer):
        return pltpu.make_async_remote_copy(
            packed.at[r, peer // SIDE], arrived.at[r, me], x_send.at[r, peer], x_recv.at[r, me],
            device_id=at_peer(peer), device_id_type=MESH,
        )

    def from_peer(r, peer):
        return pltpu.make_async_remote_copy(
            packed.at[r, peer // SIDE], arrived.at[r, peer], x_send.at[r, peer], x_recv.at[r, peer],
            device_id=at_peer(peer), device_id_type=MESH,
        )

    for r in (0, 1, 3, 2):
        lax.fori_loop(1, PLANE, lambda i, s, r=r: (to_peer(r, peer_of(i)).start(), s)[1], 0)
        arrived[r, me] = packed[r, x]

    def home(r, peer):
        return pltpu.make_async_remote_copy(
            result.at[r, peer], back.at[r, me], r_send.at[r, peer], r_recv.at[r, me],
            device_id=at_peer(peer), device_id_type=MESH,
        )

    def from_home(r, peer):
        return pltpu.make_async_remote_copy(
            result.at[r, peer], back.at[r, peer], r_send.at[r, peer], r_recv.at[r, peer],
            device_id=at_peer(peer), device_id_type=MESH,
        )

    def far_count(plane):
        falling = PEAK - ((2 * PEAK - chunks) * plane) // (DEPTH - 1)
        return jnp.where(first_core, falling, chunks - falling)

    far = far_count(zlo)
    far_next = jnp.where(last, PEAK, far_count(zlo + ahead))
    far_partner = chunks - far
    total = chunks + far
    place = jnp.where(first_core, zlo, DEPTH - 1 - zlo)
    early = 14 - 2 * place
    later = 68 - (40 * place) // 7

    def wait_partner(lo, n):
        def one(i, carry):
            on_chunk(chunk_at(i, False), lambda view: across(view(0), lo + i).wait_recv())
            return carry

        lax.fori_loop(0, n, one, 0)

    def step(u, carry):
        @pl.when(u < total)
        def _():
            near = u < chunks
            t = jnp.where(near, u, u - chunks)
            slot = jnp.where(near, side, 2)
            forward = jnp.where(
                last,
                jnp.logical_and(near, t < PEAK),
                jnp.logical_or(near, t < far_next),
            )
            target = jnp.where(last, 2, slot)
            sem = jnp.where(last, chunks + t, u)

            def act(view):
                along(view(0), view(slot), u).wait_recv()

                @pl.when(forward)
                def _():
                    along(view(slot), view(target), sem).start()

                across(view(slot), u).start()

            on_chunk(chunk_at(t), act)

        at_early, at_later, at_near, at_end = u == early, u == later, u == chunks - 1, u == total

        @pl.when(at_early | at_later | at_near | at_end)
        def _():
            r = jnp.where(at_early, 0, jnp.where(at_near, side, jnp.where(at_later, other_side, 2)))

            @pl.when(at_early & jnp.logical_not(holder) & jnp.logical_not(last))
            def _():
                for p in range(own_pieces):
                    own_to_partner(p).wait_recv()

            @pl.when(at_later)
            def _():
                wait_partner(0, chunks)

            @pl.when(at_end)
            def _():
                wait_partner(chunks, far_partner)

            lax.fori_loop(1, PLANE, lambda i, s: (from_peer(r, peer_of(i)).wait_recv(), s)[1], 0)
            inputs = arrived[r].reshape(PLANE * slots, features)
            both = jnp.dot(inputs, gu[r], preferred_element_type=jnp.float32)
            gate_act, up_act = both[:, :quarter], both[:, quarter:]
            hidden = (gate_act / (1.0 + jnp.exp(-gate_act)) * up_act).astype(jnp.bfloat16)
            part = jnp.dot(hidden, dn[r], preferred_element_type=jnp.float32)
            result[r] = part.astype(jnp.bfloat16).reshape(PLANE, slots, features)
            lax.fori_loop(1, PLANE, lambda i, s: (home(r, peer_of(i)).start(), s)[1], 0)
            back[r, me] = result[r, me]

        return carry

    lax.fori_loop(0, total + 1, step, 0)

    lane = lax.broadcasted_iota(jnp.int32, (n_tokens, PLANE * slots), 1)
    code = ((lane // (SIDE * slots)) * slots + lax.rem(lane, slots)).astype(jnp.float32)
    acc[...] = jnp.zeros_like(acc)

    def combine(r):
        lax.fori_loop(1, PLANE, lambda i, s: (from_home(r, peer_of(i)).wait_recv(), s)[1], 0)
        here = code + jnp.float32(r * SIDE * slots)
        scale = jnp.where(here == codes[0], routes[0][3], 0.0) + jnp.where(here == codes[1], routes[1][3], 0.0)
        high = scale.astype(jnp.bfloat16)
        low = (scale - high.astype(jnp.float32)).astype(jnp.bfloat16)
        values = back[r].reshape(PLANE * slots, features)
        acc[...] += jnp.dot(high, values, preferred_element_type=jnp.float32) + jnp.dot(
            low, values, preferred_element_type=jnp.float32
        )

    for r in (0, 1, 3, 2):
        combine(r)
    out_ref[...] = acc[...].astype(out_ref.dtype)

    @pl.when(holder)
    def _():
        for p in range(own_pieces):
            own_to_partner(p).wait_send()

    def sent_along(u, carry):
        on_chunk(
            chunk_at(jnp.where(u < chunks, u, u - chunks)),
            lambda view: along(view(0), view(0), u).wait_send(),
        )
        return carry

    def sent_across(u, carry):
        on_chunk(
            chunk_at(jnp.where(u < chunks, u, u - chunks)),
            lambda view: across(view(0), u).wait_send(),
        )
        return carry

    lax.fori_loop(0, chunks + far_next, sent_along, 0)
    lax.fori_loop(0, total, sent_across, 0)
    for r in range(BLOCKS):
        lax.fori_loop(1, PLANE, lambda i, s, r=r: (to_peer(r, peer_of(i)).wait_send(), s)[1], 0)
        lax.fori_loop(1, PLANE, lambda i, s, r=r: (home(r, peer_of(i)).wait_send(), s)[1], 0)


def local(tokens, expert_ids, copy_choice, gate_weights, w_gate, w_up, w_down):
    n_tokens, features = tokens.shape
    quarter = w_gate.shape[1] // 2
    slots = 2 * CAP
    chunks = features // GU_ROWS + quarter // DN_ROWS
    pieces = N_OWN + quarter // 128
    vmem = pl.BlockSpec(memory_space=pltpu.VMEM)
    anywhere = pl.BlockSpec(memory_space=pl.ANY)
    local_load = pl.pallas_call(
        load_kernel,
        out_shape=jax.ShapeDtypeStruct((8, 128), jnp.float32),
        in_specs=[vmem] * 3,
        out_specs=vmem,
    )(expert_ids, copy_choice, gate_weights)[0, : BLOCKS * SIDE]
    load = lax.psum(local_load, ("dp", "expert")) / (
        n_tokens * lax.axis_size("dp") * lax.axis_size("expert")
    )
    dma = pltpu.SemaphoreType.DMA
    grid_rows = (BLOCKS, PLANE, slots, features)
    out = pl.pallas_call(
        moe_kernel,
        out_shape=jax.ShapeDtypeStruct(tokens.shape, tokens.dtype),
        in_specs=[vmem] * 4 + [anywhere] * 3,
        out_specs=vmem,
        scratch_shapes=[
            pltpu.VMEM((BLOCKS, features, 2 * quarter), jnp.bfloat16),
            pltpu.VMEM((BLOCKS, quarter, features), jnp.bfloat16),
            pltpu.VMEM((BLOCKS, SIDE, slots, features), jnp.bfloat16),
            pltpu.VMEM(grid_rows, jnp.bfloat16),
            pltpu.VMEM(grid_rows, jnp.bfloat16),
            pltpu.VMEM(grid_rows, jnp.bfloat16),
            pltpu.VMEM((n_tokens, features), jnp.float32),
            dma((N_OWN + pieces,)),
            dma((pieces,)),
            dma((pieces,)),
            dma((chunks + PEAK,)),
            dma((chunks + PEAK,)),
            dma((chunks + PEAK,)),
            dma((chunks + PEAK,)),
            dma((BLOCKS, PLANE)),
            dma((BLOCKS, PLANE)),
            dma((BLOCKS, PLANE)),
            dma((BLOCKS, PLANE)),
        ],
        compiler_params=pltpu.CompilerParams(
            collective_id=0, has_side_effects=True, vmem_limit_bytes=56 * 1024 * 1024
        ),
        cost_estimate=pl.CostEstimate(
            flops=5_000_000_000, bytes_accessed=200_000_000, transcendentals=1_000_000
        ),
    )(tokens, expert_ids, copy_choice, gate_weights, w_gate, w_up, w_down)
    return out, load


def solution(mesh):
    return jax.shard_map(
        local,
        mesh=mesh,
        in_specs=(
            P(("dp", "expert"), None),
            P(("dp", "expert"), None),
            P(("dp", "expert"), None),
            P(("dp", "expert"), None),
            P(None, "expert"),
            P(None, "expert"),
            P("expert", None),
        ),
        out_specs=(P(("dp", "expert"), None), P()),
        check_vma=False,
    )
```

```python
import jax
import jax.numpy as jnp
from jax import lax
from jax.experimental import pallas as pl
from jax.experimental.pallas import tpu as pltpu
from jax.sharding import PartitionSpec as P

MESH = pl.DeviceIdType.MESH

BLOCKS = 4
DEPTH = 8
SIDE = 4
PLANE = SIDE * SIDE
CAP = 8
GU_ROWS = 64
DN_ROWS = 32
N_OWN = 8
REACH = 4
PEAK = 32


def routing(columns):
    rows = columns.shape[0]
    lanes = lax.broadcasted_iota(jnp.int32, (rows, 128), 1)
    ids = [columns[:, k : k + 1].astype(jnp.int32) for k in (0, 1)]
    copies = [columns[:, k + 2 : k + 3].astype(jnp.int32) for k in (0, 1)]
    hot = [(lanes == 2 * ids[k] + copies[k]).astype(jnp.float32) for k in (0, 1)]
    earlier = lax.broadcasted_iota(jnp.int32, (rows, rows), 1) < lax.broadcasted_iota(
        jnp.int32, (rows, rows), 0
    )
    before = jnp.dot(
        earlier.astype(jnp.float32).astype(jnp.bfloat16),
        (hot[0] + hot[1]).astype(jnp.bfloat16),
        preferred_element_type=jnp.float32,
    )
    ranks = [
        jnp.sum(before * hot[0], axis=1, keepdims=True),
        jnp.sum((before + hot[0]) * hot[1], axis=1, keepdims=True),
    ]
    routes = []
    for k in (0, 1):
        kept = ranks[k] < float(CAP)
        place = (copies[k] * CAP).astype(jnp.float32) + ranks[k]
        gate = jnp.where(kept, columns[:, k + 4 : k + 5], 0.0)
        routes.append((ids[k], place, kept, gate))
    return routes


def moe_kernel(
    tokens_ref, ids_ref, copy_ref, gate_ref, wg_ref, wu_ref, wd_ref, out_ref, load_ref,
    gu, dn, packed, arrived, result, back, acc, square, core_loads, chip_loads, plane_loads, other_loads, all_loads,
    own_sem, o_send, o_recv, z_send, z_recv, d_send, d_recv, x_send, x_recv, r_send, r_recv,
    c_send, c_recv, p_send, p_recv, l_send, l_recv, m_send, m_recv,
):
    dp, ex = lax.axis_index("dp"), lax.axis_index("expert")
    zlo, y = dp // SIDE, lax.rem(dp, SIDE)
    x, b, c = ex // (2 * BLOCKS), lax.rem(ex // 2, BLOCKS), lax.rem(ex, 2)
    me = x * SIDE + y
    first_core = c == 0
    features = tokens_ref.shape[1]
    quarter = dn.shape[1]
    gu_chunks = features // GU_ROWS
    chunks = gu_chunks + quarter // DN_ROWS
    own_rows = features // N_OWN
    own_pieces = N_OWN + quarter // 128
    slots = 2 * CAP

    def at_plane(step):
        z = lax.rem(b * DEPTH + zlo + step + BLOCKS * DEPTH, BLOCKS * DEPTH)
        zb, zl = z // DEPTH, lax.rem(z, DEPTH)
        return (zl * SIDE + y, x * 2 * BLOCKS + zb * 2 + c)

    def at_peer(peer):
        return (zlo * SIDE + lax.rem(peer, SIDE), (peer // SIDE) * 2 * BLOCKS + b * 2 + c)

    def peer_of(i):
        return lax.rem(me + i, PLANE)

    ahead = jnp.where(first_core, 1, -1)
    downstream = at_plane(ahead)
    partner = (dp, x * 2 * BLOCKS + b * 2 + 1 - c)

    holder = c == y // 2
    column = pl.multiple_of(lax.rem(y, 2) * quarter, 128)

    def own_copies(p):
        if p < N_OWN:
            rows = pl.ds(p * own_rows, own_rows)
            return [
                pltpu.make_async_copy(
                    w.at[rows, pl.ds(column, quarter)],
                    gu.at[0, rows, pl.ds(k * quarter, quarter)],
                    own_sem.at[2 * p + k],
                )
                for k, w in ((0, wg_ref), (1, wu_ref))
            ]
        at = (p - N_OWN) * 128
        return [
            pltpu.make_async_copy(
                wd_ref.at[pl.ds(column + at, 128), :],
                dn.at[0, pl.ds(at, 128), :],
                own_sem.at[N_OWN + p],
            )
        ]

    def own_to_partner(p):
        ref = gu.at[0, pl.ds(p * own_rows, own_rows)] if p < N_OWN else dn.at[0, pl.ds((p - N_OWN) * 128, 128)]
        return pltpu.make_async_remote_copy(
            ref, ref, o_send.at[p], o_recv.at[p], device_id=partner, device_id_type=MESH
        )

    own_order = []
    for p in range((own_pieces + 1) // 2):
        own_order += [p] if p == own_pieces - 1 - p else [p, own_pieces - 1 - p]

    @pl.when(holder)
    def _():
        for p in own_order:
            for copy in own_copies(p):
                copy.start()

    barrier = pltpu.get_barrier_semaphore()

    def greet(i, carry):
        pl.semaphore_signal(barrier, inc=1, device_id=at_peer(peer_of(i)), device_id_type=MESH)
        return carry

    for d in range(1, REACH + 1):
        pl.semaphore_signal(barrier, inc=1, device_id=at_plane(-d * ahead), device_id_type=MESH)
    pl.semaphore_signal(barrier, inc=1, device_id=partner, device_id_type=MESH)
    lax.fori_loop(1, PLANE, greet, 0)

    square[...] = jnp.zeros_like(square)
    square[0:2, :] = ids_ref[...].astype(jnp.float32)
    square[2:4, :] = copy_ref[...].astype(jnp.float32)
    square[4:6, :] = gate_ref[...]
    routes = routing(square[...].T)
    codes = []
    for expert, place, kept, _ in routes:
        group = lax.rem(b - expert + BLOCKS * SIDE, BLOCKS) * SIDE + expert // BLOCKS
        codes.append(jnp.where(kept, (group * slots).astype(jnp.float32) + place, -1.0))
    n_tokens = tokens_ref.shape[0]
    width = BLOCKS * SIDE * slots
    lanes = lax.broadcasted_iota(jnp.int32, (n_tokens, width), 1)
    plain = lanes.astype(jnp.float32)
    select = jnp.where(plain == codes[0], 1.0, 0.0) + jnp.where(plain == codes[1], 1.0, 0.0)
    rows = jnp.dot(
        select.T.astype(jnp.bfloat16), tokens_ref[...], preferred_element_type=jnp.float32
    ).astype(jnp.bfloat16)
    packed[...] = rows.reshape(packed.shape)
    experts = lax.broadcasted_iota(jnp.int32, (n_tokens, 128), 1)
    load = jnp.zeros((1, 128), jnp.float32)
    for expert, _, _, gate in routes:
        load += jnp.sum(jnp.where(experts == expert, gate, 0.0), axis=0, keepdims=True)
    core_loads[0] = jnp.broadcast_to(load, core_loads.shape[1:])

    pl.semaphore_wait(barrier, PLANE + REACH)

    core_load = pltpu.make_async_remote_copy(
        core_loads.at[0], core_loads.at[1], c_send, c_recv, device_id=partner, device_id_type=MESH
    )
    core_load.start()

    def load_to(peer):
        return pltpu.make_async_remote_copy(
            chip_loads.at[me], chip_loads.at[me], p_send.at[peer], p_recv.at[me],
            device_id=at_peer(peer), device_id_type=MESH,
        )

    def load_from(peer):
        return pltpu.make_async_remote_copy(
            chip_loads.at[peer], chip_loads.at[peer], p_send.at[peer], p_recv.at[peer],
            device_id=at_peer(peer), device_id_type=MESH,
        )

    @pl.when(holder)
    def _():
        for p in own_order:
            for copy in own_copies(p):
                copy.wait()
            own_to_partner(p).start()

    side = jnp.where(first_core, 1, 3)
    other_side = 4 - side
    last = jnp.where(first_core, zlo == DEPTH - 1, zlo == 0)

    def chunk_at(t, mine=True):
        ascending = first_core if mine else jnp.logical_not(first_core)
        return jnp.where(ascending, t, chunks - 1 - t)

    def on_chunk(chunk, act):
        @pl.when(chunk < gu_chunks)
        def _():
            act(lambda s: gu.at[s, pl.ds(pl.multiple_of(chunk * GU_ROWS, GU_ROWS), GU_ROWS)])

        @pl.when(chunk >= gu_chunks)
        def _():
            at = (chunk - gu_chunks) * DN_ROWS
            act(lambda s: dn.at[s, pl.ds(pl.multiple_of(at, DN_ROWS), DN_ROWS)])

    def along(src, dst, sem):
        return pltpu.make_async_remote_copy(
            src, dst, z_send.at[sem], z_recv.at[sem], device_id=downstream, device_id_type=MESH
        )

    def across(ref, sem):
        return pltpu.make_async_remote_copy(
            ref, ref, d_send.at[sem], d_recv.at[sem], device_id=partner, device_id_type=MESH
        )

    def send_own(t, carry):
        on_chunk(chunk_at(t), lambda view: along(view(0), view(side), t).start())
        return carry

    @pl.when(jnp.logical_and(last, holder))
    def _():
        lax.fori_loop(0, chunks, send_own, 0)

    @pl.when(jnp.logical_and(last, jnp.logical_not(holder)))
    def _():
        per_piece = chunks // own_pieces

        @pl.when(first_core)
        def _():
            for i in range(own_pieces):
                own_to_partner(i).wait_recv()
                lax.fori_loop(i * per_piece, (i + 1) * per_piece, send_own, 0)

        @pl.when(jnp.logical_not(first_core))
        def _():
            for i in range(own_pieces):
                own_to_partner(own_pieces - 1 - i).wait_recv()
                lax.fori_loop(i * per_piece, (i + 1) * per_piece, send_own, 0)

    core_load.wait_recv()
    chip_loads[me] = core_loads[0] + core_loads[1]
    lax.fori_loop(1, PLANE, lambda i, s: (load_to(peer_of(i)).start(), s)[1], 0)

    def to_peer(r, peer):
        return pltpu.make_async_remote_copy(
            packed.at[r, peer // SIDE], arrived.at[r, me], x_send.at[r, peer], x_recv.at[r, me],
            device_id=at_peer(peer), device_id_type=MESH,
        )

    def from_peer(r, peer):
        return pltpu.make_async_remote_copy(
            packed.at[r, peer // SIDE], arrived.at[r, peer], x_send.at[r, peer], x_recv.at[r, peer],
            device_id=at_peer(peer), device_id_type=MESH,
        )

    for r in (0, 1, 3, 2):
        lax.fori_loop(1, PLANE, lambda i, s, r=r: (to_peer(r, peer_of(i)).start(), s)[1], 0)
        arrived[r, me] = packed[r, x]

    def home(r, peer):
        return pltpu.make_async_remote_copy(
            result.at[r, peer], back.at[r, me], r_send.at[r, peer], r_recv.at[r, me],
            device_id=at_peer(peer), device_id_type=MESH,
        )

    def from_home(r, peer):
        return pltpu.make_async_remote_copy(
            result.at[r, peer], back.at[r, peer], r_send.at[r, peer], r_recv.at[r, peer],
            device_id=at_peer(peer), device_id_type=MESH,
        )

    def far_count(plane):
        falling = PEAK - ((2 * PEAK - chunks) * plane) // (DEPTH - 1)
        return jnp.where(first_core, falling, chunks - falling)

    planes = BLOCKS * DEPTH
    rounds = planes // 2 // REACH
    z_here = b * DEPTH + zlo
    lax.fori_loop(1, PLANE, lambda i, s: (load_from(peer_of(i)).wait_recv(), s)[1], 0)
    plane_loads[0] = jnp.sum(chip_loads[...], axis=0)

    def load_first(d):
        return pltpu.make_async_remote_copy(
            plane_loads.at[0], plane_loads.at[d], l_send.at[d - 1], l_recv.at[d - 1],
            device_id=at_plane(d * ahead), device_id_type=MESH,
        )

    def load_on(k):
        return pltpu.make_async_remote_copy(
            plane_loads.at[pl.ds((k - 1) * REACH + 1, REACH)], plane_loads.at[pl.ds(k * REACH + 1, REACH)],
            l_send.at[REACH + k - 1], l_recv.at[REACH + k - 1],
            device_id=at_plane(REACH * ahead), device_id_type=MESH,
        )

    def load_across(k):
        return pltpu.make_async_remote_copy(
            plane_loads.at[pl.ds(k * REACH + 1, REACH)], other_loads.at[pl.ds(k * REACH + 1, REACH)],
            m_send.at[k], m_recv.at[k], device_id=partner, device_id_type=MESH,
        )

    for d in range(1, REACH + 1):
        load_first(d).start()

    def load_round(k):
        if k == 1:
            for d in range(1, REACH + 1):
                load_first(d).wait_recv()
        else:
            load_on(k - 1).wait_recv()
        load_across(k - 1).start()
        if k < rounds:
            load_on(k).start()

    far = far_count(zlo)
    far_next = jnp.where(last, PEAK, far_count(zlo + ahead))
    far_partner = chunks - far
    total = chunks + far
    place = jnp.where(first_core, zlo, DEPTH - 1 - zlo)
    early = 24 - 2 * place
    later = 74 - (40 * place) // 7

    def wait_partner(lo, n):
        def one(i, carry):
            on_chunk(chunk_at(i, False), lambda view: across(view(0), lo + i).wait_recv())
            return carry

        lax.fori_loop(0, n, one, 0)

    shift = (20 * place) // 7

    def step(u, carry):
        for k, when in ((1, 20), (2, 40), (3, 58)):

            @pl.when(u == when - shift)
            def _(k=k):
                load_round(k)

        @pl.when(u < total)
        def _():
            near = u < chunks
            t = jnp.where(near, u, u - chunks)
            slot = jnp.where(near, side, 2)
            forward = jnp.where(
                last,
                jnp.logical_and(near, t < PEAK),
                jnp.logical_or(near, t < far_next),
            )
            target = jnp.where(last, 2, slot)
            sem = jnp.where(last, chunks + t, u)

            def act(view):
                along(view(0), view(slot), u).wait_recv()

                @pl.when(forward)
                def _():
                    along(view(slot), view(target), sem).start()

                across(view(slot), u).start()

            on_chunk(chunk_at(t), act)

        at_early, at_later, at_near, at_end = u == early, u == later, u == chunks - 1, u == total

        @pl.when(at_early | at_later | at_near | at_end)
        def _():
            r = jnp.where(at_early, 0, jnp.where(at_near, side, jnp.where(at_later, other_side, 2)))

            @pl.when(at_early & jnp.logical_not(holder) & jnp.logical_not(last))
            def _():
                for p in range(own_pieces):
                    own_to_partner(p).wait_recv()

            @pl.when(at_later)
            def _():
                wait_partner(0, chunks)

            @pl.when(at_end)
            def _():
                wait_partner(chunks, far_partner)

            lax.fori_loop(1, PLANE, lambda i, s: (from_peer(r, peer_of(i)).wait_recv(), s)[1], 0)
            inputs = arrived[r].reshape(PLANE * slots, features)
            both = jnp.dot(inputs, gu[r], preferred_element_type=jnp.float32)
            gate_act, up_act = both[:, :quarter], both[:, quarter:]
            hidden = (gate_act / (1.0 + jnp.exp(-gate_act)) * up_act).astype(jnp.bfloat16)
            part = jnp.dot(hidden, dn[r], preferred_element_type=jnp.float32)
            result[r] = part.astype(jnp.bfloat16).reshape(PLANE, slots, features)
            lax.fori_loop(1, PLANE, lambda i, s: (home(r, peer_of(i)).start(), s)[1], 0)
            back[r, me] = result[r, me]

        return carry

    lax.fori_loop(0, total + 1, step, 0)

    load_round(rounds)
    for k in range(rounds):
        load_across(k).wait_recv()
    for k in range(planes // 2 + 1):
        all_loads[lax.rem(z_here - k * ahead + planes, planes)] = plane_loads[k]
    for k in range(1, planes // 2):
        all_loads[lax.rem(z_here + k * ahead + planes, planes)] = other_loads[k]
    tokens_in_all = n_tokens * lax.axis_size("dp") * lax.axis_size("expert")
    load_ref[...] = jnp.sum(all_loads[...], axis=0) * (1.0 / tokens_in_all)

    lane = lax.broadcasted_iota(jnp.int32, (n_tokens, PLANE * slots), 1)
    code = ((lane // (SIDE * slots)) * slots + lax.rem(lane, slots)).astype(jnp.float32)
    acc[...] = jnp.zeros_like(acc)

    def combine(r):
        lax.fori_loop(1, PLANE, lambda i, s: (from_home(r, peer_of(i)).wait_recv(), s)[1], 0)
        here = code + jnp.float32(r * SIDE * slots)
        scale = jnp.where(here == codes[0], routes[0][3], 0.0) + jnp.where(here == codes[1], routes[1][3], 0.0)
        high = scale.astype(jnp.bfloat16)
        low = (scale - high.astype(jnp.float32)).astype(jnp.bfloat16)
        values = back[r].reshape(PLANE * slots, features)
        acc[...] += jnp.dot(high, values, preferred_element_type=jnp.float32) + jnp.dot(
            low, values, preferred_element_type=jnp.float32
        )

    for r in (0, 1, 3, 2):
        combine(r)
    out_ref[...] = acc[...].astype(out_ref.dtype)

    core_load.wait_send()
    lax.fori_loop(1, PLANE, lambda i, s: (load_to(peer_of(i)).wait_send(), s)[1], 0)
    for d in range(1, REACH + 1):
        load_first(d).wait_send()
    for k in range(1, rounds):
        load_on(k).wait_send()
    for k in range(rounds):
        load_across(k).wait_send()

    @pl.when(holder)
    def _():
        for p in range(own_pieces):
            own_to_partner(p).wait_send()

    def sent_along(u, carry):
        on_chunk(
            chunk_at(jnp.where(u < chunks, u, u - chunks)),
            lambda view: along(view(0), view(0), u).wait_send(),
        )
        return carry

    def sent_across(u, carry):
        on_chunk(
            chunk_at(jnp.where(u < chunks, u, u - chunks)),
            lambda view: across(view(0), u).wait_send(),
        )
        return carry

    lax.fori_loop(0, chunks + far_next, sent_along, 0)
    lax.fori_loop(0, total, sent_across, 0)
    for r in range(BLOCKS):
        lax.fori_loop(1, PLANE, lambda i, s, r=r: (to_peer(r, peer_of(i)).wait_send(), s)[1], 0)
        lax.fori_loop(1, PLANE, lambda i, s, r=r: (home(r, peer_of(i)).wait_send(), s)[1], 0)


def local(tokens, expert_ids, copy_choice, gate_weights, w_gate, w_up, w_down):
    n_tokens, features = tokens.shape
    quarter = w_gate.shape[1] // 2
    slots = 2 * CAP
    chunks = features // GU_ROWS + quarter // DN_ROWS
    pieces = N_OWN + quarter // 128
    vmem = pl.BlockSpec(memory_space=pltpu.VMEM)
    anywhere = pl.BlockSpec(memory_space=pl.ANY)
    dma = pltpu.SemaphoreType.DMA
    grid_rows = (BLOCKS, PLANE, slots, features)
    out, load = pl.pallas_call(
        moe_kernel,
        out_shape=[
            jax.ShapeDtypeStruct(tokens.shape, tokens.dtype),
            jax.ShapeDtypeStruct((8, 128), jnp.float32),
        ],
        in_specs=[vmem] * 4 + [anywhere] * 3,
        out_specs=[vmem] * 2,
        scratch_shapes=[
            pltpu.VMEM((BLOCKS, features, 2 * quarter), jnp.bfloat16),
            pltpu.VMEM((BLOCKS, quarter, features), jnp.bfloat16),
            pltpu.VMEM((BLOCKS, SIDE, slots, features), jnp.bfloat16),
            pltpu.VMEM(grid_rows, jnp.bfloat16),
            pltpu.VMEM(grid_rows, jnp.bfloat16),
            pltpu.VMEM(grid_rows, jnp.bfloat16),
            pltpu.VMEM((n_tokens, features), jnp.float32),
            pltpu.VMEM((n_tokens, 128), jnp.float32),
            pltpu.VMEM((2, 8, 128), jnp.float32),
            pltpu.VMEM((PLANE, 8, 128), jnp.float32),
            pltpu.VMEM((BLOCKS * DEPTH // 2 + 1, 8, 128), jnp.float32),
            pltpu.VMEM((BLOCKS * DEPTH // 2 + 1, 8, 128), jnp.float32),
            pltpu.VMEM((BLOCKS * DEPTH, 8, 128), jnp.float32),
            dma((N_OWN + pieces,)),
            dma((pieces,)),
            dma((pieces,)),
            dma((chunks + PEAK,)),
            dma((chunks + PEAK,)),
            dma((chunks + PEAK,)),
            dma((chunks + PEAK,)),
            dma((BLOCKS, PLANE)),
            dma((BLOCKS, PLANE)),
            dma((BLOCKS, PLANE)),
            dma((BLOCKS, PLANE)),
            dma,
            dma,
            dma((PLANE,)),
            dma((PLANE,)),
            dma((2 * REACH,)),
            dma((2 * REACH,)),
            dma((REACH,)),
            dma((REACH,)),
        ],
        compiler_params=pltpu.CompilerParams(
            collective_id=0, has_side_effects=True, vmem_limit_bytes=56 * 1024 * 1024
        ),
        cost_estimate=pl.CostEstimate(
            flops=5_000_000_000, bytes_accessed=200_000_000, transcendentals=1_000_000
        ),
    )(tokens, expert_ids.T, copy_choice.T, gate_weights.T, w_gate, w_up, w_down)
    return out, load[0, : BLOCKS * SIDE]


def solution(mesh):
    return jax.shard_map(
        local,
        mesh=mesh,
        in_specs=(
            P(("dp", "expert"), None),
            P(("dp", "expert"), None),
            P(("dp", "expert"), None),
            P(("dp", "expert"), None),
            P(None, "expert"),
            P(None, "expert"),
            P("expert", None),
        ),
        out_specs=(P(("dp", "expert"), None), P()),
        check_vma=False,
    )
```
